256 devices in a mesh: facet: 128 (over y, x, z), row: 2 (over core).
Axes of the slice: x: 4, y: 4, z: 8, core: 2. Of those that a mesh axis runs over, the one named last changes fastest.
Arguments:
- facet: bfloat16 [128, 2, 1024, 1024], P('facet', None, 'row'), may hold values from -6 to 6
- taper: float32 [1024], replicated, may hold values from 0.25 to 1
- shifts: int32 [128, 2, 4], P('facet'), may hold values from 0 to 1023
- cover: int32 [128, 4], P('facet'), may hold values 0 or 1
- phase: int32 [128, 4], P('facet'), may hold values from 0 to 1023
- owner: int32 [128], replicated, may hold values from 0 to 127, each once
Outputs:
- owned: float32 [128, 8, 512], P('facet', 'row')
The draws below stay inside these ranges and needn't reach their ends.
Inputs may be any that keep to these rules, and one draw needn't show every extreme that they name: owner is a permutation: every owner slot receives exactly one strip.
All inputs are finite; a program needn't handle non-finite values. No bound on the sum of `cover` on one device may be relied on, other than what follows from the above.
Results may differ from the reference program's by a relative error of at most 0.0075.
Values may be sent and summed in bfloat16 or wider, within the bound.
No kernel may reach another device: no remote copies, remote signals or barrier semaphores. Data moves between devices by JAX's collectives and lax.ppermute only.
A program may use at most 64 MiB of HBM per device.

```python
import math
import jax
import jax.numpy as jnp
from jax import lax

F = 1024
SG = 256
NSUB = 4
FACETS = 128
STRIP_ROWS = 4
N_FACET = 128
N_ROW = 2


def plant(array, stream_key, least, high):
    longest = array.shape.index(max(array.shape))
    spots = []
    for shift in (0, 1):
        where = [jax.random.randint(jax.random.fold_in(stream_key, axis), (), 0, length) for axis, length in enumerate(array.shape)]
        where[longest] = (where[longest] + shift) % array.shape[longest]
        spots.append(tuple(where))
    return array.at[spots[0]].set(least).at[spots[1]].set(high)


def block_scale(own_key, dims, pieces, smallest, high):
    def one(axis_at, blocks):
        heights = jax.random.uniform(jax.random.fold_in(jax.random.fold_in(own_key, 6), axis_at), (blocks,), jnp.float32, smallest / len(pieces), high / len(pieces))
        return jnp.repeat(jnp.exp(heights), dims[axis_at] // blocks).reshape((-1,) + (1,) * (len(dims) - axis_at - 1))

    level = one(*pieces[0])
    for cut in pieces[1:]:
        level = level * one(*cut)
    return level


def bell_draw(key, dims, spread, reach, pieces=(), held_as=jnp.bfloat16):
    array = spread * jax.random.normal(key, dims, jnp.float32)
    if pieces:
        array = array * block_scale(key, dims, pieces, -0.22, 0.18)
    return jnp.clip(array, -reach, reach).astype(held_as)


def setup_inputs(seed: int = 0) -> dict:
    key_list = jax.random.split(jax.random.key(seed), 7)
    return {
        "facet": bell_draw(key_list[0], (FACETS, 2, F, F), 1.0, 6.0, ((0, 128), (2, 2))),
        "taper": jnp.clip(jnp.exp(jax.random.uniform(key_list[1], (F,), jnp.float32, math.log(0.25), math.log(1.0))), 0.25, 1.0),
        "shifts": plant(jax.random.randint(key_list[2], (FACETS, 2, NSUB), 0, F), jax.random.fold_in(key_list[2], 1), 0, F - 1).astype(jnp.int32),
        "cover": plant((jax.random.randint(key_list[3], (FACETS, NSUB), 0, 4) < 3).astype(jnp.int32), jax.random.fold_in(key_list[3], 1), 0, 1),
        "phase": plant(jax.random.randint(key_list[4], (FACETS, NSUB), 0, F), jax.random.fold_in(key_list[4], 1), 0, F - 1).astype(jnp.int32),
        "owner": jax.random.permutation(key_list[5], N_FACET).astype(jnp.int32),
    }


def tables(shift, columns, taper_part):
    freqs = jnp.arange(SG, dtype=jnp.int32)
    index = (shift + freqs)[:, None] * columns[None, :] % F
    angles = index.astype(jnp.float32) * (2.0 * math.pi / F)
    weights = taper_part[None, :] / math.sqrt(F)
    return jnp.stack([jnp.cos(angles) * weights, -jnp.sin(angles) * weights], axis=0).astype(jnp.bfloat16)

def mixer_of(v_tab):
    top = jnp.concatenate([v_tab[0], -v_tab[1]], axis=1)
    bottom = jnp.concatenate([v_tab[1], v_tab[0]], axis=1)
    return jnp.concatenate([top, bottom], axis=0)

def first_pass(u_tab, facet_rows):
    products = jnp.einsum('ajx,bxy->abjy', u_tab.astype(jnp.float32), facet_rows.astype(jnp.float32), precision=lax.Precision.HIGHEST)
    real = products[0, 0] - products[1, 1]
    imag = products[0, 1] + products[1, 0]
    return jnp.concatenate([real, imag], axis=1).astype(jnp.bfloat16)

def rotate(image, cover_value, phase_value):
    angle = phase_value.astype(jnp.float32) * (2.0 * math.pi / F)
    cos_w = cover_value.astype(jnp.float32) * jnp.cos(angle)
    sin_w = cover_value.astype(jnp.float32) * jnp.sin(angle)
    real = image[:, :SG]
    imag = image[:, SG:]
    return jnp.concatenate([cos_w * real - sin_w * imag, sin_w * real + cos_w * imag], axis=1)

def reference(facet, taper, shifts, cover, phase, owner):
    half = F // N_ROW
    all_columns = jnp.arange(F, dtype=jnp.int32)

    def one_facet(total, items):
        facet_one, shift_one, cover_one, phase_one = items
        images = []
        for subgrid in range(NSUB):
            u_tab = tables(shift_one[0, subgrid], all_columns, taper)
            mixer = mixer_of(tables(shift_one[1, subgrid], all_columns, taper)).astype(jnp.float32)
            image = jnp.zeros((SG, 2 * SG), jnp.float32)
            for part_index in range(N_ROW):
                low = part_index * half
                partial_value = first_pass(u_tab[:, :, low:low + half], facet_one[:, low:low + half, :])
                image = image + jnp.einsum('jy,ky->jk', partial_value.astype(jnp.float32), mixer, precision=lax.Precision.HIGHEST)
            images.append(rotate(image, cover_one[subgrid], phase_one[subgrid]))
        return (total + jnp.stack(images), None)
    start_total = jnp.zeros((NSUB, SG, 2 * SG), jnp.float32)
    total, _ = lax.scan(one_facet, start_total, (facet, shifts, cover, phase))
    blocks = SG // N_ROW // STRIP_ROWS
    strips = total.reshape(NSUB, N_ROW, blocks, STRIP_ROWS, 2 * SG).transpose(1, 0, 2, 3, 4)
    strips = strips.reshape(N_ROW, N_FACET, STRIP_ROWS, 2 * SG)
    positions = jnp.arange(N_FACET, dtype=jnp.int32)
    inverse = jnp.zeros((N_FACET,), jnp.int32).at[owner].set(positions)
    return strips[:, inverse].transpose(1, 0, 2, 3).reshape(N_FACET, N_ROW * STRIP_ROWS, 2 * SG)
```

```python
import math

import jax
import jax.numpy as jnp
from jax import lax
from jax.experimental import pallas as pl
from jax.experimental.pallas import tpu as pltpu
from jax.sharding import PartitionSpec as P

F = 1024
SG = 256
NSUB = 4
RADIX = 4
Q = F // RADIX
J = SG // RADIX
HALF = J // 2
STRIPS = NSUB * HALF
ROWS = 16
LANES = 128
STEP = 2.0 * math.pi / F
BF = jnp.bfloat16
F32 = jnp.float32


def unit(index):
    angle = (index & (F - 1)).astype(F32) * STEP
    return jnp.cos(angle), -jnp.sin(angle)


def iota(shape, axis):
    return lax.broadcasted_iota(jnp.int32, shape, axis)


def by_subgrid(values, shape):
    group = iota(shape, 0) // RADIX
    out = jnp.full(shape, values[0])
    for s in range(1, NSUB):
        out = jnp.where(group == s, values[s], out)
    return out


def images(shifts, cover, phase, owner, half, taper, facet_hbm, keep, send,
           facet, grid, left, right, part, strips, columns, sem):
    copies = [
        pltpu.make_async_copy(facet_hbm.at[0, part_at], facet.at[part_at], sem.at[part_at])
        for part_at in range(2)
    ]
    for copy in copies:
        copy.start()
    h = half[0]

    low_r, low_i = unit(4 * iota((8, Q), 0) * iota((8, Q), 1))
    high_r, high_i = unit(32 * iota((8, Q), 0) * iota((8, Q), 1))
    comb_r = jnp.concatenate([low_r * high_r[u:u + 1] - low_i * high_i[u:u + 1] for u in range(J // 8)])
    comb_i = jnp.concatenate([low_r * high_i[u:u + 1] + low_i * high_r[u:u + 1] for u in range(J // 8)])
    shape = (NSUB * RADIX, Q)
    scale = 1.0 / math.sqrt(F)

    def write(table, at, row, rr, ri):
        re = comb_r * rr - comb_i * ri
        im = comb_r * ri + comb_i * rr
        re_b, im_b = re.astype(BF), im.astype(BF)
        table[at, row:row + J, :Q] = re_b
        table[at, row:row + J, Q:] = (-im).astype(BF)
        table[at, row + J:row + 2 * J, :Q] = im_b
        table[at, row + J:row + 2 * J, Q:] = re_b

    freq = by_subgrid([shifts[0, 0, s] for s in range(NSUB)], shape) + iota(shape, 0) % RADIX
    turn = by_subgrid([phase[0, s] for s in range(NSUB)], shape)
    gain = by_subgrid([cover[0, s].astype(F32) * scale for s in range(NSUB)], shape)
    row_r, row_i = unit(freq * (iota(shape, 1) + h * (F // 2)) - turn)
    row_r, row_i = row_r * gain, row_i * gain
    for s in range(NSUB):
        for t in range(RADIX):
            n = s * RADIX + t
            write(left, (shifts[0, 0, s] + t) & 3, s * 2 * J, row_r[n:n + 1], row_i[n:n + 1])
    freq = by_subgrid([shifts[0, 1, s] for s in range(NSUB)], shape) + iota(shape, 0) % RADIX
    row_r, row_i = unit(freq * iota(shape, 1))
    row_r, row_i = row_r * scale, row_i * scale
    for n in range(NSUB * RADIX):
        write(right, n, 0, row_r[n:n + 1], row_i[n:n + 1])

    for q in range(F // 2 // LANES):
        row = taper[pl.ds(h * 4 + q, 1), :]
        columns[q * LANES:(q + 1) * LANES, :] = jnp.transpose(jnp.broadcast_to(row, (LANES, LANES)))

    for copy in copies:
        copy.wait()

    rows = 16
    for v in range(Q // LANES):
        across = [jnp.broadcast_to(taper[2 * a + v:2 * a + v + 1, :], (rows, LANES)) for a in range(RADIX)]

        def block(i, carry):
            b = pl.multiple_of(i * rows, rows)
            lines = []
            for a in range(2):
                down = columns[pl.ds(a * Q + b, rows), :]
                z = []
                for c in range(RADIX):
                    weight = down * across[c]
                    lane = c * Q + v * LANES
                    z.append([
                        facet[p, pl.ds(a * Q + b, rows), lane:lane + LANES].astype(F32) * weight
                        for p in range(2)
                    ])
                e0 = [z[0][p] + z[2][p] for p in range(2)]
                e1 = [z[0][p] - z[2][p] for p in range(2)]
                o0 = [z[1][p] + z[3][p] for p in range(2)]
                o1 = [z[1][p] - z[3][p] for p in range(2)]
                lines.append([
                    (e0[0] + o0[0], e0[1] + o0[1]),
                    (e1[0] + o1[1], e1[1] - o1[0]),
                    (e0[0] - o0[0], e0[1] - o0[1]),
                    (e1[0] - o1[1], e1[1] + o1[0]),
                ])
            for c in range(RADIX):
                (ar, ai), (br, bi) = lines[0][c], lines[1][c]
                lane = c * Q + v * LANES
                outs = [(ar + br, ai + bi), (ar + bi, ai - br), (ar - br, ai - bi), (ar - bi, ai + br)]
                for x, pair in enumerate(outs):
                    for p in range(2):
                        grid[x, pl.ds(p * Q + b, rows), lane:lane + LANES] = pair[p].astype(BF)
            return carry

        lax.fori_loop(0, Q // rows, block, 0)

    for c in range(RADIX):
        slots = [(c - shifts[0, 0, s]) & 3 for s in range(NSUB)]
        for y in range(RADIX):
            sums = jnp.dot(left[c], grid[c, :, y * Q:(y + 1) * Q], preferred_element_type=F32).astype(BF)
            for s in range(NSUB):
                for p in range(2):
                    row = (2 * s + p) * J
                    part[s, slots[s], :, (2 * y + p) * Q:(2 * y + p + 1) * Q] = sums[row:row + J]

    for s in range(NSUB):
        for k in range(RADIX):
            lane = pl.multiple_of(((shifts[0, 1, s] + k) & 3) * (2 * Q), 2 * Q)
            rows_in = part[s, :, :, pl.ds(lane, 2 * Q)].reshape(SG, 2 * Q)
            image = lax.dot_general(rows_in, right[s * RADIX + k], (((1,), (1,)), ((), ())),
                                    preferred_element_type=F32)
            for t in range(RADIX):
                for r in range(2):
                    start = (r * NSUB + s) * HALF * ROWS + k * RADIX + t
                    row = t * J + r * HALF
                    strips[pl.ds(start, HALF, stride=ROWS), :] = image[row:row + HALF]

    def place(k, carry):
        to = owner[k]
        mine = pl.multiple_of((h * STRIPS + k) * ROWS, ROWS)
        theirs = pl.multiple_of(((1 - h) * STRIPS + k) * ROWS, ROWS)
        keep[to] = strips[pl.ds(mine, ROWS), :]
        send[to] = strips[pl.ds(theirs, ROWS), :].astype(BF)
        return carry

    lax.fori_loop(0, STRIPS, place, 0, unroll=8)


def total(parts, out):
    sums = parts[0].astype(F32)
    for i in range(1, parts.shape[0]):
        sums = sums + parts[i].astype(F32)
    lane, col = iota((LANES, 2 * SG), 0), iota((LANES, 2 * SG), 1)
    spread = (col == (lane // J) * SG + (lane % J) * RADIX).astype(F32)
    wide = jnp.dot(sums, spread, precision=lax.Precision.HIGHEST, preferred_element_type=F32)
    result = wide[:RADIX]
    for k in range(1, RADIX):
        result = result + pltpu.roll(wide[k * RADIX:(k + 1) * RADIX], k, 1)
    out[0] = result


def per_device(facet, taper, shifts, cover, phase, owner):
    smem = pl.BlockSpec(memory_space=pltpu.SMEM)
    vmem = pl.BlockSpec(memory_space=pltpu.VMEM)
    half = lax.axis_index("row").reshape(1)
    keep, send = pl.pallas_call(
        images,
        out_shape=(
            jax.ShapeDtypeStruct((STRIPS, ROWS, LANES), F32),
            jax.ShapeDtypeStruct((STRIPS, ROWS, LANES), BF),
        ),
        in_specs=[smem] * 5 + [vmem, pl.BlockSpec(memory_space=pl.ANY)],
        out_specs=(vmem, vmem),
        scratch_shapes=[
            pltpu.VMEM((2, F // 2, F), BF),
            pltpu.VMEM((RADIX, 2 * Q, F), BF),
            pltpu.VMEM((RADIX, NSUB * 2 * J, 2 * Q), BF),
            pltpu.VMEM((NSUB * RADIX, 2 * J, 2 * Q), BF),
            pltpu.VMEM((NSUB, RADIX, J, 2 * F), BF),
            pltpu.VMEM((2 * STRIPS * ROWS, LANES), F32),
            pltpu.VMEM((F // 2, LANES), F32),
            pltpu.SemaphoreType.DMA((2,)),
        ],
        compiler_params=pltpu.CompilerParams(vmem_limit_bytes=40 * 2**20),
        name="images",
    )(shifts, cover, phase, owner, half, taper.reshape(8, LANES), facet)
    with jax.named_scope("row_swap"):
        other = lax.ppermute(send, "row", [(0, 1), (1, 0)])
        merged = (keep + other.astype(F32)).astype(BF)
    with jax.named_scope("to_owners"):
        parts = lax.all_to_all(merged, "facet", split_axis=0, concat_axis=0, tiled=True)
    return pl.pallas_call(
        total,
        out_shape=jax.ShapeDtypeStruct((1, RADIX, 2 * SG), F32),
        in_specs=[vmem],
        out_specs=vmem,
        name="total",
    )(parts)


def solution(mesh):
    return jax.shard_map(
        per_device,
        mesh=mesh,
        in_specs=(
            P("facet", None, "row", None),
            P(),
            P("facet", None, None),
            P("facet", None),
            P("facet", None),
            P(),
        ),
        out_specs=P("facet", "row", None),
        check_vma=False,
    )
```

```python
import math

import jax
import jax.numpy as jnp
from jax import lax
from jax.experimental import pallas as pl
from jax.experimental.pallas import tpu as pltpu
from jax.sharding import PartitionSpec as P

F = 1024
SG = 256
NSUB = 4
RADIX = 4
Q = F // RADIX
J = SG // RADIX
HALF = J // 2
STRIPS = NSUB * HALF
ROWS = 16
LANES = 128
STEP = 2.0 * math.pi / F
BF = jnp.bfloat16
F32 = jnp.float32


def unit(index):
    angle = (index & (F - 1)).astype(F32) * STEP
    return jnp.cos(angle), -jnp.sin(angle)


def iota(shape, axis):
    return lax.broadcasted_iota(jnp.int32, shape, axis)


def by_subgrid(values, shape):
    group = iota(shape, 0) // RADIX
    out = jnp.full(shape, values[0])
    for s in range(1, NSUB):
        out = jnp.where(group == s, values[s], out)
    return out


def images(shifts_in, cover_in, phase_in, owner_in, taper_in, facet_in, keep, send,
           shifts, cover, phase, owner, taper, facet, grid, left, right, part, strips, columns, sem):
    moves = [(shifts_in, shifts), (cover_in, cover), (phase_in, phase), (owner_in, owner), (taper_in, taper)]
    small = [pltpu.make_async_copy(src, dst, sem.at[n]) for n, (src, dst) in enumerate(moves)]
    copies = [
        pltpu.make_async_copy(facet_in.at[0, p], facet.at[p], sem.at[len(moves) + p]) for p in range(2)
    ]
    for copy in small + copies:
        copy.start()
    h = lax.axis_index("row")

    low_r, low_i = unit(4 * iota((8, Q), 0) * iota((8, Q), 1))
    high_r, high_i = unit(32 * iota((8, Q), 0) * iota((8, Q), 1))
    comb_r = jnp.concatenate([low_r * high_r[u:u + 1] - low_i * high_i[u:u + 1] for u in range(J // 8)])
    comb_i = jnp.concatenate([low_r * high_i[u:u + 1] + low_i * high_r[u:u + 1] for u in range(J // 8)])
    shape = (NSUB * RADIX, Q)
    scale = 1.0 / math.sqrt(F)

    def write(table, at, row, rr, ri):
        re = comb_r * rr - comb_i * ri
        im = comb_r * ri + comb_i * rr
        re_b, im_b = re.astype(BF), im.astype(BF)
        table[at, row:row + J, :Q] = re_b
        table[at, row:row + J, Q:] = (-im).astype(BF)
        table[at, row + J:row + 2 * J, :Q] = im_b
        table[at, row + J:row + 2 * J, Q:] = re_b

    for copy in small:
        copy.wait()
    freq = by_subgrid([shifts[0, 0, s] for s in range(NSUB)], shape) + iota(shape, 0) % RADIX
    turn = by_subgrid([phase[0, s] for s in range(NSUB)], shape)
    gain = by_subgrid([cover[0, s].astype(F32) * scale for s in range(NSUB)], shape)
    row_r, row_i = unit(freq * (iota(shape, 1) + h * (F // 2)) - turn)
    row_r, row_i = row_r * gain, row_i * gain
    for s in range(NSUB):
        for t in range(RADIX):
            n = s * RADIX + t
            write(left, (shifts[0, 0, s] + t) & 3, s * 2 * J, row_r[n:n + 1], row_i[n:n + 1])
    freq = by_subgrid([shifts[0, 1, s] for s in range(NSUB)], shape) + iota(shape, 0) % RADIX
    row_r, row_i = unit(freq * iota(shape, 1))
    row_r, row_i = row_r * scale, row_i * scale
    for n in range(NSUB * RADIX):
        at = n // RADIX * RADIX + ((shifts[0, 1, n // RADIX] + n) & 3)
        write(right, at, 0, row_r[n:n + 1], row_i[n:n + 1])

    for q in range(F // 2 // LANES):
        row = taper[pl.ds(h * 4 + q, 1), :]
        columns[q * LANES:(q + 1) * LANES, :] = jnp.transpose(jnp.broadcast_to(row, (LANES, LANES)))

    for copy in copies:
        copy.wait()

    def butterfly(b, v, across):
        lines = []
        for a in range(2):
            down = columns[pl.ds(a * Q + b, ROWS), :]
            z = []
            for c in range(RADIX):
                weight = down * across[c]
                lane = c * Q + v * LANES
                z.append([
                    facet[p, pl.ds(a * Q + b, ROWS), lane:lane + LANES].astype(F32) * weight
                    for p in range(2)
                ])
            e0 = [z[0][p] + z[2][p] for p in range(2)]
            e1 = [z[0][p] - z[2][p] for p in range(2)]
            o0 = [z[1][p] + z[3][p] for p in range(2)]
            o1 = [z[1][p] - z[3][p] for p in range(2)]
            lines.append([
                (e0[0] + o0[0], e0[1] + o0[1]),
                (e1[0] + o1[1], e1[1] - o1[0]),
                (e0[0] - o0[0], e0[1] - o0[1]),
                (e1[0] - o1[1], e1[1] + o1[0]),
            ])
        for c in range(RADIX):
            (ar, ai), (br, bi) = lines[0][c], lines[1][c]
            lane = (v * RADIX + c) * LANES
            outs = [(ar + br, ai + bi), (ar + bi, ai - br), (ar - br, ai - bi), (ar - bi, ai + br)]
            for x, pair in enumerate(outs):
                for p in range(2):
                    grid[x, pl.ds(p * Q + b, ROWS), lane:lane + LANES] = pair[p].astype(BF)

    def first(c, v, y):
        lane = (v * RADIX + y) * LANES
        sums = jnp.dot(left[c], grid[c, :, lane:lane + 2 * LANES], preferred_element_type=F32).astype(BF)
        for s in range(NSUB):
            for p in range(2):
                row = (2 * s + p) * J
                for i in range(2):
                    to = (2 * (y + i) + p) * Q + v * LANES
                    part[s, c, :, to:to + LANES] = sums[row:row + J, i * LANES:(i + 1) * LANES]

    def rim(v):
        return [jnp.broadcast_to(taper[2 * a + v:2 * a + v + 1, :], (ROWS, LANES)) for a in range(RADIX)]

    blocks = Q // ROWS
    edges = rim(0)

    def step(i, carry):
        butterfly(pl.multiple_of(i * ROWS, ROWS), 0, edges)
        return carry

    lax.fori_loop(0, blocks, step, 0, unroll=4)
    tiles = [(c, y) for c in range(RADIX) for y in (0, 2)]
    edges = rim(1)
    if True:
        for n, (c, y) in enumerate(tiles):
            for i in range(n * blocks // 8, (n + 1) * blocks // 8):
                butterfly(i * ROWS, 1, edges)
            first(c, 0, y)
    else:
        def step1(i, carry):
            butterfly(pl.multiple_of(i * ROWS, ROWS), 1, edges)
            return carry
        lax.fori_loop(0, blocks, step1, 0, unroll=4)
        for c, y in tiles:
            first(c, 0, y)
    for c, y in tiles:
        first(c, 1, y)

    for s in range(NSUB):
        for y in range(RADIX):
            k = (y - shifts[0, 1, s]) & 3
            rows_in = part[s, :, :, 2 * Q * y:2 * Q * (y + 1)].reshape(SG, 2 * Q)
            image = lax.dot_general(rows_in, right[s * RADIX + y], (((1,), (1,)), ((), ())),
                                    preferred_element_type=F32)
            for c in range(RADIX):
                t = (c - shifts[0, 0, s]) & 3
                for r in range(2):
                    start = r * HALF * ROWS + k * RADIX + t
                    row = c * J + r * HALF
                    strips[s, pl.ds(start, HALF, stride=ROWS), :] = image[row:row + HALF]
        for b in range(HALF):
            to = owner[s * HALF + b]
            mine = pl.multiple_of((h * HALF + b) * ROWS, ROWS)
            theirs = pl.multiple_of(((1 - h) * HALF + b) * ROWS, ROWS)
            keep[to] = strips[s, pl.ds(mine, ROWS), :]
            send[to] = strips[s, pl.ds(theirs, ROWS), :].astype(BF)


def total(parts_in, out, parts, sem):
    half = STRIPS // 2
    copies = [
        pltpu.make_async_copy(parts_in.at[pl.ds(i * half, half)], parts.at[pl.ds(i * half, half)], sem.at[i])
        for i in range(2)
    ]
    for copy in copies:
        copy.start()
    lane, col = iota((LANES, 2 * SG), 0), iota((LANES, 2 * SG), 1)
    spread = (col == (lane // J) * SG + (lane % J) * RADIX).astype(F32).astype(BF)
    sums = [jnp.zeros((ROWS, LANES), F32)] * 8
    for i in range(STRIPS):
        if i % half == 0:
            copies[i // half].wait()
        sums[i % 8] = sums[i % 8] + parts[i].astype(F32)
    while len(sums) > 1:
        sums = [a + b for a, b in zip(sums[::2], sums[1::2])]
    high = sums[0].astype(BF)
    rest = sums[0] - high.astype(F32)
    middle = rest.astype(BF)
    low = (rest - middle.astype(F32)).astype(BF)
    wide = jnp.dot(jnp.concatenate([high, middle, low]), spread, preferred_element_type=F32)
    wide = wide[:ROWS] + (wide[ROWS:2 * ROWS] + wide[2 * ROWS:])
    result = wide[:RADIX]
    for k in range(1, RADIX):
        result = result + pltpu.roll(wide[k * RADIX:(k + 1) * RADIX], k, 1)
    out[0] = result


def per_device(facet, taper, shifts, cover, phase, owner):
    anywhere = pl.BlockSpec(memory_space=pl.ANY)
    vmem = pl.BlockSpec(memory_space=pltpu.VMEM)
    strips = (STRIPS, ROWS, LANES)
    given = [
        pltpu.with_memory_space_constraint(x, pltpu.HBM)
        for x in (shifts, cover, phase, owner, taper.reshape(8, LANES), facet)
    ]
    keep, send = pl.pallas_call(
        images,
        out_shape=(jax.ShapeDtypeStruct(strips, F32), jax.ShapeDtypeStruct(strips, BF)),
        in_specs=[anywhere] * 6,
        out_specs=(vmem, vmem),
        scratch_shapes=[
            pltpu.SMEM(shifts.shape, jnp.int32),
            pltpu.SMEM(cover.shape, jnp.int32),
            pltpu.SMEM(phase.shape, jnp.int32),
            pltpu.SMEM(owner.shape, jnp.int32),
            pltpu.VMEM((8, LANES), F32),
            pltpu.VMEM((2, F // 2, F), BF),
            pltpu.VMEM((RADIX, 2 * Q, F), BF),
            pltpu.VMEM((RADIX, NSUB * 2 * J, 2 * Q), BF),
            pltpu.VMEM((NSUB * RADIX, 2 * J, 2 * Q), BF),
            pltpu.VMEM((NSUB, RADIX, J, 2 * F), BF),
            pltpu.VMEM((NSUB, SG // RADIX * ROWS, LANES), F32),
            pltpu.VMEM((F // 2, LANES), F32),
            pltpu.SemaphoreType.DMA((7,)),
        ],
        compiler_params=pltpu.CompilerParams(vmem_limit_bytes=40 * 2**20),
        name="images",
    )(*given)
    with jax.named_scope("row_swap"):
        other = lax.ppermute(send, "row", [(0, 1), (1, 0)])
        merged = (keep + other.astype(F32)).astype(BF)
    with jax.named_scope("to_owners"):
        parts = lax.all_to_all(merged, "facet", split_axis=0, concat_axis=0, tiled=True)
    return pl.pallas_call(
        total,
        out_shape=jax.ShapeDtypeStruct((1, RADIX, 2 * SG), F32),
        in_specs=[anywhere],
        out_specs=vmem,
        scratch_shapes=[pltpu.VMEM(strips, BF), pltpu.SemaphoreType.DMA((2,))],
        name="total",
    )(parts)


def solution(mesh):
    return jax.shard_map(
        per_device,
        mesh=mesh,
        in_specs=(
            P("facet", None, "row", None),
            P(),
            P("facet", None, None),
            P("facet", None),
            P("facet", None),
            P(),
        ),
        out_specs=P("facet", "row", None),
        check_vma=False,
    )
```

```python
import math

import jax
import jax.numpy as jnp
from jax import lax
from jax.experimental import pallas as pl
from jax.experimental.pallas import tpu as pltpu
from jax.sharding import Mesh, PartitionSpec as P

F = 1024
SG = 256
NSUB = 4
RADIX = 4
Q = F // RADIX
J = SG // RADIX
HALF = J // 2
STRIPS = NSUB * HALF
ROWS = 16
LANES = 128
STEP = 2.0 * math.pi / F
BF = jnp.bfloat16
F32 = jnp.float32


def unit(index):
    angle = (index & (F - 1)).astype(F32) * STEP
    return jnp.cos(angle), -jnp.sin(angle)


def iota(shape, axis):
    return lax.broadcasted_iota(jnp.int32, shape, axis)


def by_subgrid(values, shape):
    group = iota(shape, 0) // RADIX
    out = jnp.full(shape, values[0])
    for s in range(1, NSUB):
        out = jnp.where(group == s, values[s], out)
    return out


def images(shifts_in, cover_in, phase_in, owner_in, taper_in, facet_in, keep, send,
           shifts, cover, phase, owner, taper, facet, grid, left, right, part, strips, columns, sem):
    moves = [(shifts_in, shifts), (cover_in, cover), (phase_in, phase), (owner_in, owner), (taper_in, taper)]
    small = [pltpu.make_async_copy(src, dst, sem.at[n]) for n, (src, dst) in enumerate(moves)]
    copies = [
        pltpu.make_async_copy(facet_in.at[0, p], facet.at[p], sem.at[len(moves) + p]) for p in range(2)
    ]
    for copy in small + copies:
        copy.start()
    h = lax.axis_index("row")

    low_r, low_i = unit(4 * iota((8, Q), 0) * iota((8, Q), 1))
    high_r, high_i = unit(32 * iota((8, Q), 0) * iota((8, Q), 1))
    comb_r = jnp.concatenate([low_r * high_r[u:u + 1] - low_i * high_i[u:u + 1] for u in range(J // 8)])
    comb_i = jnp.concatenate([low_r * high_i[u:u + 1] + low_i * high_r[u:u + 1] for u in range(J // 8)])
    shape = (NSUB * RADIX, Q)
    scale = 1.0 / math.sqrt(F)

    def write(table, at, row, rr, ri):
        re = comb_r * rr - comb_i * ri
        im = comb_r * ri + comb_i * rr
        re_b, im_b = re.astype(BF), im.astype(BF)
        table[at, row:row + J, :Q] = re_b
        table[at, row:row + J, Q:] = (-im).astype(BF)
        table[at, row + J:row + 2 * J, :Q] = im_b
        table[at, row + J:row + 2 * J, Q:] = re_b

    for copy in small:
        copy.wait()
    freq = by_subgrid([shifts[0, 0, s] for s in range(NSUB)], shape) + iota(shape, 0) % RADIX
    turn = by_subgrid([phase[0, s] for s in range(NSUB)], shape)
    gain = by_subgrid([cover[0, s].astype(F32) * scale for s in range(NSUB)], shape)
    row_r, row_i = unit(freq * (iota(shape, 1) + h * (F // 2)) - turn)
    row_r, row_i = row_r * gain, row_i * gain
    for s in range(NSUB):
        for t in range(RADIX):
            n = s * RADIX + t
            write(left, (shifts[0, 0, s] + t) & 3, s * 2 * J, row_r[n:n + 1], row_i[n:n + 1])
    freq = by_subgrid([shifts[0, 1, s] for s in range(NSUB)], shape) + iota(shape, 0) % RADIX
    row_r, row_i = unit(freq * iota(shape, 1))
    row_r, row_i = row_r * scale, row_i * scale
    for n in range(NSUB * RADIX):
        at = n // RADIX * RADIX + ((shifts[0, 1, n // RADIX] + n) & 3)
        write(right, at, 0, row_r[n:n + 1], row_i[n:n + 1])

    for q in range(F // 2 // LANES):
        row = taper[pl.ds(h * 4 + q, 1), :]
        columns[q * LANES:(q + 1) * LANES, :] = jnp.transpose(jnp.broadcast_to(row, (LANES, LANES)))

    for copy in copies:
        copy.wait()

    def butterfly(b, v, across):
        lines = []
        for a in range(2):
            down = columns[pl.ds(a * Q + b, ROWS), :]
            z = []
            for c in range(RADIX):
                weight = down * across[c]
                lane = c * Q + v * LANES
                z.append([
                    facet[p, pl.ds(a * Q + b, ROWS), lane:lane + LANES].astype(F32) * weight
                    for p in range(2)
                ])
            e0 = [z[0][p] + z[2][p] for p in range(2)]
            e1 = [z[0][p] - z[2][p] for p in range(2)]
            o0 = [z[1][p] + z[3][p] for p in range(2)]
            o1 = [z[1][p] - z[3][p] for p in range(2)]
            lines.append([
                (e0[0] + o0[0], e0[1] + o0[1]),
                (e1[0] + o1[1], e1[1] - o1[0]),
                (e0[0] - o0[0], e0[1] - o0[1]),
                (e1[0] - o1[1], e1[1] + o1[0]),
            ])
        for c in range(RADIX):
            (ar, ai), (br, bi) = lines[0][c], lines[1][c]
            lane = (v * RADIX + c) * LANES
            outs = [(ar + br, ai + bi), (ar + bi, ai - br), (ar - br, ai - bi), (ar - bi, ai + br)]
            for x, pair in enumerate(outs):
                for p in range(2):
                    grid[x, pl.ds(p * Q + b, ROWS), lane:lane + LANES] = pair[p].astype(BF)

    def first(c, v, y):
        lane = (v * RADIX + y) * LANES
        sums = jnp.dot(left[c], grid[c, :, lane:lane + 2 * LANES], preferred_element_type=F32).astype(BF)
        for s in range(NSUB):
            for p in range(2):
                row = (2 * s + p) * J
                for i in range(2):
                    to = (2 * (y + i) + p) * Q + v * LANES
                    part[s, c, :, to:to + LANES] = sums[row:row + J, i * LANES:(i + 1) * LANES]

    def rim(v):
        return [jnp.broadcast_to(taper[2 * a + v:2 * a + v + 1, :], (ROWS, LANES)) for a in range(RADIX)]

    blocks = Q // ROWS
    edges = rim(0)

    def step(i, carry):
        butterfly(pl.multiple_of(i * ROWS, ROWS), 0, edges)
        return carry

    lax.fori_loop(0, blocks, step, 0, unroll=4)
    tiles = [(c, y) for c in range(RADIX) for y in (0, 2)]
    edges = rim(1)
    if True:
        for n, (c, y) in enumerate(tiles):
            for i in range(n * blocks // 8, (n + 1) * blocks // 8):
                butterfly(i * ROWS, 1, edges)
            first(c, 0, y)
    else:
        def step1(i, carry):
            butterfly(pl.multiple_of(i * ROWS, ROWS), 1, edges)
            return carry
        lax.fori_loop(0, blocks, step1, 0, unroll=4)
        for c, y in tiles:
            first(c, 0, y)
    for c, y in tiles:
        first(c, 1, y)

    for s in range(NSUB):
        for y in range(RADIX):
            k = (y - shifts[0, 1, s]) & 3
            rows_in = part[s, :, :, 2 * Q * y:2 * Q * (y + 1)].reshape(SG, 2 * Q)
            image = lax.dot_general(rows_in, right[s * RADIX + y], (((1,), (1,)), ((), ())),
                                    preferred_element_type=F32)
            for c in range(RADIX):
                t = (c - shifts[0, 0, s]) & 3
                for r in range(2):
                    start = r * HALF * ROWS + k * RADIX + t
                    row = c * J + r * HALF
                    strips[s, pl.ds(start, HALF, stride=ROWS), :] = image[row:row + HALF]
        for b in range(HALF):
            to = owner[s * HALF + b]
            mine = pl.multiple_of((h * HALF + b) * ROWS, ROWS)
            theirs = pl.multiple_of(((1 - h) * HALF + b) * ROWS, ROWS)
            keep[to] = strips[s, pl.ds(mine, ROWS), :]
            send[to] = strips[s, pl.ds(theirs, ROWS), :].astype(BF)


def column(parts, out):
    depth = out.shape[0]
    for z in range(depth):
        sums = [parts[i + z].astype(F32) for i in range(0, STRIPS, depth)]
        while len(sums) > 1:
            sums = [a + b for a, b in zip(sums[::2], sums[1::2])]
        out[z] = sums[0].astype(BF)


def total(parts, out):
    lane, col = iota((LANES, 2 * SG), 0), iota((LANES, 2 * SG), 1)
    spread = (col == (lane // J) * SG + (lane % J) * RADIX).astype(F32).astype(BF)
    sums = [parts[i].astype(F32) for i in range(parts.shape[0])]
    while len(sums) > 1:
        sums = [a + b for a, b in zip(sums[::2], sums[1::2])]
    high = sums[0].astype(BF)
    rest = sums[0] - high.astype(F32)
    middle = rest.astype(BF)
    low = (rest - middle.astype(F32)).astype(BF)
    wide = jnp.dot(jnp.concatenate([high, middle, low]), spread, preferred_element_type=F32)
    wide = wide[:ROWS] + (wide[ROWS:2 * ROWS] + wide[2 * ROWS:])
    result = wide[:RADIX]
    for k in range(1, RADIX):
        result = result + pltpu.roll(wide[k * RADIX:(k + 1) * RADIX], k, 1)
    out[0] = result


def per_device(facet, taper, shifts, cover, phase, owner):
    anywhere = pl.BlockSpec(memory_space=pl.ANY)
    vmem = pl.BlockSpec(memory_space=pltpu.VMEM)
    strips = (STRIPS, ROWS, LANES)
    given = [
        pltpu.with_memory_space_constraint(x, pltpu.HBM)
        for x in (shifts, cover, phase, owner, taper.reshape(8, LANES), facet)
    ]
    keep, send = pl.pallas_call(
        images,
        out_shape=(jax.ShapeDtypeStruct(strips, F32), jax.ShapeDtypeStruct(strips, BF)),
        in_specs=[anywhere] * 6,
        out_specs=(vmem, vmem),
        scratch_shapes=[
            pltpu.SMEM(shifts.shape, jnp.int32),
            pltpu.SMEM(cover.shape, jnp.int32),
            pltpu.SMEM(phase.shape, jnp.int32),
            pltpu.SMEM(owner.shape, jnp.int32),
            pltpu.VMEM((8, LANES), F32),
            pltpu.VMEM((2, F // 2, F), BF),
            pltpu.VMEM((RADIX, 2 * Q, F), BF),
            pltpu.VMEM((RADIX, NSUB * 2 * J, 2 * Q), BF),
            pltpu.VMEM((NSUB * RADIX, 2 * J, 2 * Q), BF),
            pltpu.VMEM((NSUB, RADIX, J, 2 * F), BF),
            pltpu.VMEM((NSUB, SG // RADIX * ROWS, LANES), F32),
            pltpu.VMEM((F // 2, LANES), F32),
            pltpu.SemaphoreType.DMA((7,)),
        ],
        compiler_params=pltpu.CompilerParams(vmem_limit_bytes=40 * 2**20),
        name="images",
    )(*given)
    with jax.named_scope("row_swap"):
        other = lax.ppermute(send, "row", [(0, 1), (1, 0)])
        merged = (keep + other.astype(F32)).astype(BF)
    with jax.named_scope("to_columns"):
        parts = lax.all_to_all(merged, "plane", split_axis=0, concat_axis=0, tiled=True)
    depth = lax.axis_size("line")
    summed = pl.pallas_call(
        column,
        out_shape=jax.ShapeDtypeStruct((depth, ROWS, LANES), BF),
        in_specs=[vmem],
        out_specs=vmem,
        name="column",
    )(pltpu.with_memory_space_constraint(parts, pltpu.VMEM))
    with jax.named_scope("to_owners"):
        parts = lax.all_to_all(summed, "line", split_axis=0, concat_axis=0, tiled=True)
    return pl.pallas_call(
        total,
        out_shape=jax.ShapeDtypeStruct((1, RADIX, 2 * SG), F32),
        in_specs=[vmem],
        out_specs=vmem,
        name="total",
    )(pltpu.with_memory_space_constraint(parts, pltpu.VMEM))


def solution(mesh):
    line = 8
    grid = Mesh(mesh.devices.reshape(-1, line, mesh.devices.shape[1]), ("plane", "line", "row"))
    facet = ("plane", "line")
    return jax.shard_map(
        per_device,
        mesh=grid,
        in_specs=(
            P(facet, None, "row", None),
            P(),
            P(facet, None, None),
            P(facet, None),
            P(facet, None),
            P(),
        ),
        out_specs=P(facet, "row", None),
        check_vma=False,
    )
```

```python
import math

import jax
import jax.numpy as jnp
from jax import lax
from jax.experimental import pallas as pl
from jax.experimental.pallas import tpu as pltpu
from jax.sharding import Mesh, PartitionSpec as P

F = 1024
SG = 256
NSUB = 4
RADIX = 4
Q = F // RADIX
J = SG // RADIX
HALF = J // 2
STRIPS = NSUB * HALF
ROWS = 16
LANES = 128
STEP = 2.0 * math.pi / F
CHUNKS = 4
BF = jnp.bfloat16
F32 = jnp.float32


def unit(index):
    angle = (index & (F - 1)).astype(F32) * STEP
    return jnp.cos(angle), -jnp.sin(angle)


def iota(shape, axis):
    return lax.broadcasted_iota(jnp.int32, shape, axis)


def by_subgrid(values, shape):
    group = iota(shape, 0) // RADIX
    out = jnp.full(shape, values[0])
    for s in range(1, NSUB):
        out = jnp.where(group == s, values[s], out)
    return out


def second(half, shifts, owner, right, part, strips, out):
    for s in range(NSUB):
        for y in range(RADIX):
            k = (y - shifts[0, 1, s]) & 3
            rows = pl.ds(pl.multiple_of(half * HALF, HALF), HALF)
            rows_in = part[s, :, rows, 2 * Q * y:2 * Q * (y + 1)].reshape(SG // 2, 2 * Q)
            image = lax.dot_general(rows_in, right[s * RADIX + y], (((1,), (1,)), ((), ())),
                                    preferred_element_type=F32)
            for c in range(RADIX):
                t = (c - shifts[0, 0, s]) & 3
                strips[s, pl.ds(k * RADIX + t, HALF, stride=ROWS), :] = image[c * HALF:(c + 1) * HALF]
        for b in range(HALF):
            out[owner[s * HALF + b]] = strips[s, b * ROWS:(b + 1) * ROWS, :].astype(out.dtype)


def images(shifts_in, cover_in, phase_in, owner_in, taper_in, facet_in, send, part, right,
           shifts, cover, phase, owner, taper, facet, grid, left, strips, columns, sem):
    moves = [(shifts_in, shifts), (cover_in, cover), (phase_in, phase), (owner_in, owner), (taper_in, taper)]
    small = [pltpu.make_async_copy(src, dst, sem.at[n]) for n, (src, dst) in enumerate(moves)]
    copies = []
    for g in range(CHUNKS):
        for p in range(2):
            for a in range(2):
                rows = pl.ds(a * Q + g * Q // CHUNKS, Q // CHUNKS)
                n = len(moves) + len(copies)
                copies.append(pltpu.make_async_copy(facet_in.at[0, p, rows], facet.at[p, rows], sem.at[n]))
    for copy in small + copies:
        copy.start()
    h = lax.axis_index("row")

    low_r, low_i = unit(4 * iota((8, Q), 0) * iota((8, Q), 1))
    high_r, high_i = unit(32 * iota((8, Q), 0) * iota((8, Q), 1))
    comb_r = jnp.concatenate([low_r * high_r[u:u + 1] - low_i * high_i[u:u + 1] for u in range(J // 8)])
    comb_i = jnp.concatenate([low_r * high_i[u:u + 1] + low_i * high_r[u:u + 1] for u in range(J // 8)])
    shape = (NSUB * RADIX, Q)
    scale = 1.0 / math.sqrt(F)

    def write(table, at, row, rr, ri):
        re = comb_r * rr - comb_i * ri
        im = comb_r * ri + comb_i * rr
        re_b, im_b = re.astype(BF), im.astype(BF)
        table[at, row:row + J, :Q] = re_b
        table[at, row:row + J, Q:] = (-im).astype(BF)
        table[at, row + J:row + 2 * J, :Q] = im_b
        table[at, row + J:row + 2 * J, Q:] = re_b

    for copy in small:
        copy.wait()
    freq = by_subgrid([shifts[0, 0, s] for s in range(NSUB)], shape) + iota(shape, 0) % RADIX
    turn = by_subgrid([phase[0, s] for s in range(NSUB)], shape)
    gain = by_subgrid([cover[0, s].astype(F32) * scale for s in range(NSUB)], shape)
    row_r, row_i = unit(freq * (iota(shape, 1) + h * (F // 2)) - turn)
    row_r, row_i = row_r * gain, row_i * gain
    for s in range(NSUB):
        for t in range(RADIX):
            n = s * RADIX + t
            write(left, (shifts[0, 0, s] + t) & 3, s * 2 * J, row_r[n:n + 1], row_i[n:n + 1])
    freq = by_subgrid([shifts[0, 1, s] for s in range(NSUB)], shape) + iota(shape, 0) % RADIX
    row_r, row_i = unit(freq * iota(shape, 1))
    row_r, row_i = row_r * scale, row_i * scale
    for n in range(NSUB * RADIX):
        at = n // RADIX * RADIX + ((shifts[0, 1, n // RADIX] + n) & 3)
        write(right, at, 0, row_r[n:n + 1], row_i[n:n + 1])

    for q in range(F // 2 // LANES):
        row = taper[pl.ds(h * 4 + q, 1), :]
        columns[q * LANES:(q + 1) * LANES, :] = jnp.transpose(jnp.broadcast_to(row, (LANES, LANES)))

    def butterfly(b, v, across):
        lines = []
        for a in range(2):
            down = columns[pl.ds(a * Q + b, ROWS), :]
            z = []
            for c in range(RADIX):
                weight = down * across[c]
                lane = c * Q + v * LANES
                z.append([
                    facet[p, pl.ds(a * Q + b, ROWS), lane:lane + LANES].astype(F32) * weight
                    for p in range(2)
                ])
            e0 = [z[0][p] + z[2][p] for p in range(2)]
            e1 = [z[0][p] - z[2][p] for p in range(2)]
            o0 = [z[1][p] + z[3][p] for p in range(2)]
            o1 = [z[1][p] - z[3][p] for p in range(2)]
            lines.append([
                (e0[0] + o0[0], e0[1] + o0[1]),
                (e1[0] + o1[1], e1[1] - o1[0]),
                (e0[0] - o0[0], e0[1] - o0[1]),
                (e1[0] - o1[1], e1[1] + o1[0]),
            ])
        for c in range(RADIX):
            (ar, ai), (br, bi) = lines[0][c], lines[1][c]
            lane = (v * RADIX + c) * LANES
            outs = [(ar + br, ai + bi), (ar + bi, ai - br), (ar - br, ai - bi), (ar - bi, ai + br)]
            for x, pair in enumerate(outs):
                for p in range(2):
                    grid[x, pl.ds(p * Q + b, ROWS), lane:lane + LANES] = pair[p].astype(BF)

    def first(c, v, y):
        lane = (v * RADIX + y) * LANES
        sums = jnp.dot(left[c], grid[c, :, lane:lane + 2 * LANES], preferred_element_type=F32).astype(BF)
        for s in range(NSUB):
            for p in range(2):
                row = (2 * s + p) * J
                for i in range(2):
                    to = (2 * (y + i) + p) * Q + v * LANES
                    part[s, c, :, to:to + LANES] = sums[row:row + J, i * LANES:(i + 1) * LANES]

    def rim(v):
        return [jnp.broadcast_to(taper[2 * a + v:2 * a + v + 1, :], (ROWS, LANES)) for a in range(RADIX)]

    blocks = Q // ROWS
    edges = rim(0)

    def step(i, carry):
        butterfly(pl.multiple_of(i * ROWS, ROWS), 0, edges)
        return carry

    for g in range(CHUNKS):
        for copy in copies[4 * g:4 * g + 4]:
            copy.wait()
        lax.fori_loop(g * blocks // CHUNKS, (g + 1) * blocks // CHUNKS, step, 0, unroll=4)
    tiles = [(c, y) for c in range(RADIX) for y in (0, 2)]
    edges = rim(1)
    if True:
        for n, (c, y) in enumerate(tiles):
            for i in range(n * blocks // 8, (n + 1) * blocks // 8):
                butterfly(i * ROWS, 1, edges)
            first(c, 0, y)
    else:
        def step1(i, carry):
            butterfly(pl.multiple_of(i * ROWS, ROWS), 1, edges)
            return carry
        lax.fori_loop(0, blocks, step1, 0, unroll=4)
        for c, y in tiles:
            first(c, 0, y)
    for c, y in tiles:
        first(c, 1, y)

    second(1 - h, shifts, owner, right, part, strips, send)


def kept(shifts_in, owner_in, right, part, keep, shifts, owner, strips, sem):
    copies = [
        pltpu.make_async_copy(src, dst, sem.at[n])
        for n, (src, dst) in enumerate([(shifts_in, shifts), (owner_in, owner)])
    ]
    for copy in copies:
        copy.start()
    for copy in copies:
        copy.wait()
    second(lax.axis_index("row"), shifts, owner, right, part, strips, keep)


def column(parts, out):
    depth = out.shape[0]
    for z in range(depth):
        sums = [parts[i + z].astype(F32) for i in range(0, STRIPS, depth)]
        while len(sums) > 1:
            sums = [a + b for a, b in zip(sums[::2], sums[1::2])]
        out[z] = sums[0].astype(BF)


def total(parts, out):
    lane, col = iota((LANES, 2 * SG), 0), iota((LANES, 2 * SG), 1)
    spread = (col == (lane // J) * SG + (lane % J) * RADIX).astype(F32).astype(BF)
    sums = [parts[i].astype(F32) for i in range(parts.shape[0])]
    while len(sums) > 1:
        sums = [a + b for a, b in zip(sums[::2], sums[1::2])]
    high = sums[0].astype(BF)
    rest = sums[0] - high.astype(F32)
    middle = rest.astype(BF)
    low = (rest - middle.astype(F32)).astype(BF)
    wide = jnp.dot(jnp.concatenate([high, middle, low]), spread, preferred_element_type=F32)
    wide = wide[:ROWS] + (wide[ROWS:2 * ROWS] + wide[2 * ROWS:])
    result = wide[:RADIX]
    for k in range(1, RADIX):
        result = result + pltpu.roll(wide[k * RADIX:(k + 1) * RADIX], k, 1)
    out[0] = result


def per_device(facet, taper, shifts, cover, phase, owner):
    anywhere = pl.BlockSpec(memory_space=pl.ANY)
    vmem = pl.BlockSpec(memory_space=pltpu.VMEM)
    strips = (STRIPS, ROWS, LANES)
    given = [
        pltpu.with_memory_space_constraint(x, pltpu.HBM)
        for x in (shifts, cover, phase, owner, taper.reshape(8, LANES), facet)
    ]
    held = pltpu.VMEM((NSUB, HALF * ROWS, LANES), F32)
    send, part, right = pl.pallas_call(
        images,
        out_shape=(
            jax.ShapeDtypeStruct(strips, BF),
            jax.ShapeDtypeStruct((NSUB, RADIX, J, 2 * F), BF),
            jax.ShapeDtypeStruct((NSUB * RADIX, 2 * J, 2 * Q), BF),
        ),
        in_specs=[anywhere] * 6,
        out_specs=(vmem, vmem, vmem),
        scratch_shapes=[
            pltpu.SMEM(shifts.shape, jnp.int32),
            pltpu.SMEM(cover.shape, jnp.int32),
            pltpu.SMEM(phase.shape, jnp.int32),
            pltpu.SMEM(owner.shape, jnp.int32),
            pltpu.VMEM((8, LANES), F32),
            pltpu.VMEM((2, F // 2, F), BF),
            pltpu.VMEM((RADIX, 2 * Q, F), BF),
            pltpu.VMEM((RADIX, NSUB * 2 * J, 2 * Q), BF),
            held,
            pltpu.VMEM((F // 2, LANES), F32),
            pltpu.SemaphoreType.DMA((5 + 4 * CHUNKS,)),
        ],
        compiler_params=pltpu.CompilerParams(vmem_limit_bytes=32 * 2**20),
        name="images",
    )(*given)
    with jax.named_scope("row_swap"):
        other = lax.ppermute(send, "row", [(0, 1), (1, 0)])
    work = 2 * STRIPS * ROWS * LANES * 2 * Q
    keep = pl.pallas_call(
        kept,
        out_shape=jax.ShapeDtypeStruct(strips, F32),
        in_specs=[anywhere, anywhere, vmem, vmem],
        out_specs=vmem,
        scratch_shapes=[
            pltpu.SMEM(shifts.shape, jnp.int32),
            pltpu.SMEM(owner.shape, jnp.int32),
            held,
            pltpu.SemaphoreType.DMA((2,)),
        ],
        compiler_params=pltpu.CompilerParams(vmem_limit_bytes=16 * 2**20),
        cost_estimate=pl.CostEstimate(flops=work, bytes_accessed=6 * 2**20, transcendentals=0),
        name="kept",
    )(given[0], given[3], *(pltpu.with_memory_space_constraint(x, pltpu.VMEM) for x in (right, part)))
    with jax.named_scope("row_swap"):
        merged = (keep + other.astype(F32)).astype(BF)
    with jax.named_scope("to_columns"):
        parts = lax.all_to_all(merged, "plane", split_axis=0, concat_axis=0, tiled=True)
    depth = lax.axis_size("line")
    summed = pl.pallas_call(
        column,
        out_shape=pltpu.VMEM((depth, ROWS, LANES), BF),
        in_specs=[vmem],
        out_specs=vmem,
        name="column",
    )(pltpu.with_memory_space_constraint(parts, pltpu.VMEM))
    with jax.named_scope("to_owners"):
        parts = lax.all_to_all(summed, "line", split_axis=0, concat_axis=0, tiled=True)
    return pl.pallas_call(
        total,
        out_shape=jax.ShapeDtypeStruct((1, RADIX, 2 * SG), F32),
        in_specs=[vmem],
        out_specs=vmem,
        name="total",
    )(pltpu.with_memory_space_constraint(parts, pltpu.VMEM))


def solution(mesh):
    line = 8
    grid = Mesh(mesh.devices.reshape(-1, line, mesh.devices.shape[1]), ("plane", "line", "row"))
    facet = ("plane", "line")
    return jax.shard_map(
        per_device,
        mesh=grid,
        in_specs=(
            P(facet, None, "row", None),
            P(),
            P(facet, None, None),
            P(facet, None),
            P(facet, None),
            P(),
        ),
        out_specs=P(facet, "row", None),
        check_vma=False,
    )
```

```python
import math

import jax
import jax.numpy as jnp
from jax import lax
from jax.experimental import pallas as pl
from jax.experimental.pallas import tpu as pltpu
from jax.sharding import Mesh, PartitionSpec as P

F = 1024
SG = 256
NSUB = 4
RADIX = 4
Q = F // RADIX
J = SG // RADIX
HALF = J // 2
STRIPS = NSUB * HALF
ROWS = 16
LANES = 128
STEP = 2.0 * math.pi / F
BF = jnp.bfloat16
F32 = jnp.float32


def unit(index):
    angle = (index & (F - 1)).astype(F32) * STEP
    return jnp.cos(angle), -jnp.sin(angle)


def iota(shape, axis):
    return lax.broadcasted_iota(jnp.int32, shape, axis)


def by_subgrid(values, shape):
    group = iota(shape, 0) // RADIX
    out = jnp.full(shape, values[0])
    for s in range(1, NSUB):
        out = jnp.where(group == s, values[s], out)
    return out


def second(half, shifts, owner, right, part, strips, out):
    for s in range(NSUB):
        for y in range(RADIX):
            k = (y - shifts[0, 1, s]) & 3
            rows = pl.ds(pl.multiple_of(half * HALF, HALF), HALF)
            rows_in = part[s, :, rows, 2 * Q * y:2 * Q * (y + 1)].reshape(SG // 2, 2 * Q)
            image = lax.dot_general(rows_in, right[s * RADIX + y], (((1,), (1,)), ((), ())),
                                    preferred_element_type=F32)
            for c in range(RADIX):
                t = (c - shifts[0, 0, s]) & 3
                strips[s, pl.ds(k * RADIX + t, HALF, stride=ROWS), :] = image[c * HALF:(c + 1) * HALF]
        for b in range(HALF):
            out[owner[s * HALF + b]] = strips[s, b * ROWS:(b + 1) * ROWS, :].astype(out.dtype)


def images(shifts_in, cover_in, phase_in, owner_in, taper_in, facet_in, send, part, right,
           shifts, cover, phase, owner, taper, facet, grid, left, strips, columns, sem):
    moves = [(shifts_in, shifts), (cover_in, cover), (phase_in, phase), (owner_in, owner), (taper_in, taper)]
    small = [pltpu.make_async_copy(src, dst, sem.at[n]) for n, (src, dst) in enumerate(moves)]
    copies = [
        pltpu.make_async_copy(facet_in.at[0, p], facet.at[p], sem.at[len(moves) + p]) for p in range(2)
    ]
    for copy in small + copies:
        copy.start()
    h = lax.axis_index("row")

    low_r, low_i = unit(4 * iota((8, Q), 0) * iota((8, Q), 1))
    high_r, high_i = unit(32 * iota((8, Q), 0) * iota((8, Q), 1))
    comb_r = jnp.concatenate([low_r * high_r[u:u + 1] - low_i * high_i[u:u + 1] for u in range(J // 8)])
    comb_i = jnp.concatenate([low_r * high_i[u:u + 1] + low_i * high_r[u:u + 1] for u in range(J // 8)])
    shape = (NSUB * RADIX, Q)
    scale = 1.0 / math.sqrt(F)

    def write(table, at, row, rr, ri):
        re = comb_r * rr - comb_i * ri
        im = comb_r * ri + comb_i * rr
        re_b, im_b = re.astype(BF), im.astype(BF)
        table[at, row:row + J, :Q] = re_b
        table[at, row:row + J, Q:] = (-im).astype(BF)
        table[at, row + J:row + 2 * J, :Q] = im_b
        table[at, row + J:row + 2 * J, Q:] = re_b

    for copy in small:
        copy.wait()
    freq = by_subgrid([shifts[0, 0, s] for s in range(NSUB)], shape) + iota(shape, 0) % RADIX
    turn = by_subgrid([phase[0, s] for s in range(NSUB)], shape)
    gain = by_subgrid([cover[0, s].astype(F32) * scale for s in range(NSUB)], shape)
    row_r, row_i = unit(freq * (iota(shape, 1) + h * (F // 2)) - turn)
    row_r, row_i = row_r * gain, row_i * gain
    for s in range(NSUB):
        for t in range(RADIX):
            n = s * RADIX + t
            write(left, (shifts[0, 0, s] + t) & 3, s * 2 * J, row_r[n:n + 1], row_i[n:n + 1])
    freq = by_subgrid([shifts[0, 1, s] for s in range(NSUB)], shape) + iota(shape, 0) % RADIX
    row_r, row_i = unit(freq * iota(shape, 1))
    row_r, row_i = row_r * scale, row_i * scale
    for n in range(NSUB * RADIX):
        at = n // RADIX * RADIX + ((shifts[0, 1, n // RADIX] + n) & 3)
        write(right, at, 0, row_r[n:n + 1], row_i[n:n + 1])

    for q in range(F // 2 // LANES):
        row = taper[pl.ds(h * 4 + q, 1), :]
        columns[q * LANES:(q + 1) * LANES, :] = jnp.transpose(jnp.broadcast_to(row, (LANES, LANES)))

    def butterfly(b, v, across):
        lines = []
        for a in range(2):
            down = columns[pl.ds(a * Q + b, ROWS), :]
            z = []
            for c in range(RADIX):
                weight = down * across[c]
                lane = c * Q + v * LANES
                z.append([
                    facet[p, pl.ds(a * Q + b, ROWS), lane:lane + LANES].astype(F32) * weight
                    for p in range(2)
                ])
            e0 = [z[0][p] + z[2][p] for p in range(2)]
            e1 = [z[0][p] - z[2][p] for p in range(2)]
            o0 = [z[1][p] + z[3][p] for p in range(2)]
            o1 = [z[1][p] - z[3][p] for p in range(2)]
            lines.append([
                (e0[0] + o0[0], e0[1] + o0[1]),
                (e1[0] + o1[1], e1[1] - o1[0]),
                (e0[0] - o0[0], e0[1] - o0[1]),
                (e1[0] - o1[1], e1[1] + o1[0]),
            ])
        for c in range(RADIX):
            (ar, ai), (br, bi) = lines[0][c], lines[1][c]
            lane = (v * RADIX + c) * LANES
            outs = [(ar + br, ai + bi), (ar + bi, ai - br), (ar - br, ai - bi), (ar - bi, ai + br)]
            for x, pair in enumerate(outs):
                for p in range(2):
                    grid[x, pl.ds(p * Q + b, ROWS), lane:lane + LANES] = pair[p].astype(BF)

    def first(c, v, y):
        lane = (v * RADIX + y) * LANES
        sums = jnp.dot(left[c], grid[c, :, lane:lane + 2 * LANES], preferred_element_type=F32).astype(BF)
        for s in range(NSUB):
            for p in range(2):
                row = (2 * s + p) * J
                for i in range(2):
                    to = (2 * (y + i) + p) * Q + v * LANES
                    part[s, c, :, to:to + LANES] = sums[row:row + J, i * LANES:(i + 1) * LANES]

    def rim(v):
        return [jnp.broadcast_to(taper[2 * a + v:2 * a + v + 1, :], (ROWS, LANES)) for a in range(RADIX)]

    blocks = Q // ROWS
    edges = rim(0)
    for copy in copies:
        copy.wait()
    for i in range(blocks):
        butterfly(i * ROWS, 0, edges)
    tiles = [(c, y) for c in range(RADIX) for y in (0, 2)]
    edges = rim(1)
    for n, (c, y) in enumerate(tiles):
        for i in range(n * blocks // len(tiles), (n + 1) * blocks // len(tiles)):
            butterfly(i * ROWS, 1, edges)
        first(c, 0, y)
    for c, y in tiles:
        first(c, 1, y)

    second(1 - h, shifts, owner, right, part, strips, send)


def kept(shifts_in, owner_in, right, part, keep, shifts, owner, strips, sem):
    copies = [
        pltpu.make_async_copy(src, dst, sem.at[n])
        for n, (src, dst) in enumerate([(shifts_in, shifts), (owner_in, owner)])
    ]
    for copy in copies:
        copy.start()
    for copy in copies:
        copy.wait()
    second(lax.axis_index("row"), shifts, owner, right, part, strips, keep)


def column(parts, out):
    depth = out.shape[0]
    for z in range(depth):
        sums = [parts[i + z].astype(F32) for i in range(0, STRIPS, depth)]
        while len(sums) > 1:
            sums = [a + b for a, b in zip(sums[::2], sums[1::2])]
        out[z] = sums[0].astype(BF)


def total(parts, out):
    lane, col = iota((LANES, 2 * SG), 0), iota((LANES, 2 * SG), 1)
    spread = (col == (lane // J) * SG + (lane % J) * RADIX).astype(F32).astype(BF)
    sums = [parts[i].astype(F32) for i in range(parts.shape[0])]
    while len(sums) > 1:
        sums = [a + b for a, b in zip(sums[::2], sums[1::2])]
    high = sums[0].astype(BF)
    rest = sums[0] - high.astype(F32)
    middle = rest.astype(BF)
    low = (rest - middle.astype(F32)).astype(BF)
    wide = jnp.dot(jnp.concatenate([high, middle, low]), spread, preferred_element_type=F32)
    wide = wide[:ROWS] + (wide[ROWS:2 * ROWS] + wide[2 * ROWS:])
    result = wide[:RADIX]
    for k in range(1, RADIX):
        result = result + pltpu.roll(wide[k * RADIX:(k + 1) * RADIX], k, 1)
    out[0] = result


def per_device(facet, taper, shifts, cover, phase, owner):
    anywhere = pl.BlockSpec(memory_space=pl.ANY)
    vmem = pl.BlockSpec(memory_space=pltpu.VMEM)
    strips = (STRIPS, ROWS, LANES)
    given = [
        pltpu.with_memory_space_constraint(x, pltpu.HBM)
        for x in (shifts, cover, phase, owner, taper.reshape(8, LANES), facet)
    ]
    held = pltpu.VMEM((NSUB, HALF * ROWS, LANES), F32)
    send, part, right = pl.pallas_call(
        images,
        out_shape=(
            jax.ShapeDtypeStruct(strips, BF),
            jax.ShapeDtypeStruct((NSUB, RADIX, J, 2 * F), BF),
            jax.ShapeDtypeStruct((NSUB * RADIX, 2 * J, 2 * Q), BF),
        ),
        in_specs=[anywhere] * 6,
        out_specs=(vmem, vmem, vmem),
        scratch_shapes=[
            pltpu.SMEM(shifts.shape, jnp.int32),
            pltpu.SMEM(cover.shape, jnp.int32),
            pltpu.SMEM(phase.shape, jnp.int32),
            pltpu.SMEM(owner.shape, jnp.int32),
            pltpu.VMEM((8, LANES), F32),
            pltpu.VMEM((2, F // 2, F), BF),
            pltpu.VMEM((RADIX, 2 * Q, F), BF),
            pltpu.VMEM((RADIX, NSUB * 2 * J, 2 * Q), BF),
            held,
            pltpu.VMEM((F // 2, LANES), F32),
            pltpu.SemaphoreType.DMA((7,)),
        ],
        compiler_params=pltpu.CompilerParams(vmem_limit_bytes=32 * 2**20),
        name="images",
    )(*given)
    with jax.named_scope("row_swap"):
        other = lax.ppermute(send, "row", [(0, 1), (1, 0)])
    work = 2 * STRIPS * ROWS * LANES * 2 * Q
    keep = pl.pallas_call(
        kept,
        out_shape=jax.ShapeDtypeStruct(strips, F32),
        in_specs=[anywhere, anywhere, vmem, vmem],
        out_specs=vmem,
        scratch_shapes=[
            pltpu.SMEM(shifts.shape, jnp.int32),
            pltpu.SMEM(owner.shape, jnp.int32),
            held,
            pltpu.SemaphoreType.DMA((2,)),
        ],
        compiler_params=pltpu.CompilerParams(vmem_limit_bytes=16 * 2**20),
        cost_estimate=pl.CostEstimate(flops=work, bytes_accessed=6 * 2**20, transcendentals=0),
        name="kept",
    )(given[0], given[3], *(pltpu.with_memory_space_constraint(x, pltpu.VMEM) for x in (right, part)))
    with jax.named_scope("row_swap"):
        merged = (keep + other.astype(F32)).astype(BF)
    with jax.named_scope("to_columns"):
        parts = lax.all_to_all(merged, "plane", split_axis=0, concat_axis=0, tiled=True)
    depth = lax.axis_size("line")
    summed = pl.pallas_call(
        column,
        out_shape=pltpu.VMEM((depth, ROWS, LANES), BF),
        in_specs=[vmem],
        out_specs=vmem,
        name="column",
    )(pltpu.with_memory_space_constraint(parts, pltpu.VMEM))
    with jax.named_scope("to_owners"):
        parts = lax.all_to_all(summed, "line", split_axis=0, concat_axis=0, tiled=True)
    return pl.pallas_call(
        total,
        out_shape=jax.ShapeDtypeStruct((1, RADIX, 2 * SG), F32),
        in_specs=[vmem],
        out_specs=vmem,
        name="total",
    )(pltpu.with_memory_space_constraint(parts, pltpu.VMEM))


def solution(mesh):
    line = 8
    grid = Mesh(mesh.devices.reshape(-1, line, mesh.devices.shape[1]), ("plane", "line", "row"))
    facet = ("plane", "line")
    return jax.shard_map(
        per_device,
        mesh=grid,
        in_specs=(
            P(facet, None, "row", None),
            P(),
            P(facet, None, None),
            P(facet, None),
            P(facet, None),
            P(),
        ),
        out_specs=P(facet, "row", None),
        check_vma=False,
    )
```

```python
import math

import jax
import jax.numpy as jnp
from jax import lax
from jax.experimental import pallas as pl
from jax.experimental.pallas import tpu as pltpu
from jax.sharding import Mesh, PartitionSpec as P

F = 1024
SG = 256
NSUB = 4
RADIX = 4
Q = F // RADIX
J = SG // RADIX
HALF = J // 2
STRIPS = NSUB * HALF
ROWS = 16
LANES = 128
STEP = 2.0 * math.pi / F
BF = jnp.bfloat16
F32 = jnp.float32


def unit(index):
    angle = (index & (F - 1)).astype(F32) * STEP
    return jnp.cos(angle), -jnp.sin(angle)


def iota(shape, axis):
    return lax.broadcasted_iota(jnp.int32, shape, axis)


def by_subgrid(values, shape):
    group = iota(shape, 0) // RADIX
    out = jnp.full(shape, values[0])
    for s in range(1, NSUB):
        out = jnp.where(group == s, values[s], out)
    return out


def second(half, shifts, owner, right, part, strips, out):
    for s in range(NSUB):
        for y in range(RADIX):
            k = (y - shifts[0, 1, s]) & 3
            rows = pl.ds(pl.multiple_of(half * HALF, HALF), HALF)
            rows_in = part[s, :, rows, 2 * Q * y:2 * Q * (y + 1)].reshape(SG // 2, 2 * Q)
            image = lax.dot_general(rows_in, right[s * RADIX + y], (((1,), (1,)), ((), ())),
                                    preferred_element_type=F32)
            for c in range(RADIX):
                t = (c - shifts[0, 0, s]) & 3
                strips[s, pl.ds(k * RADIX + t, HALF, stride=ROWS), :] = image[c * HALF:(c + 1) * HALF]
        for b in range(HALF):
            out[owner[s * HALF + b]] = strips[s, b * ROWS:(b + 1) * ROWS, :].astype(out.dtype)


def images(shifts_in, cover_in, phase_in, owner_in, taper_in, facet_in, send, part, right,
           shifts, cover, phase, owner, taper, facet, grid, left, strips, columns, sem):
    moves = [(shifts_in, shifts), (cover_in, cover), (phase_in, phase), (owner_in, owner), (taper_in, taper)]
    small = [pltpu.make_async_copy(src, dst, sem.at[n]) for n, (src, dst) in enumerate(moves)]
    copies = [
        pltpu.make_async_copy(facet_in.at[0, p], facet.at[p], sem.at[len(moves) + p]) for p in range(2)
    ]
    for copy in small + copies:
        copy.start()
    h = lax.axis_index("row")

    low_r, low_i = unit(4 * iota((8, Q), 0) * iota((8, Q), 1))
    high_r, high_i = unit(32 * iota((8, Q), 0) * iota((8, Q), 1))
    comb_r = jnp.concatenate([low_r * high_r[u:u + 1] - low_i * high_i[u:u + 1] for u in range(J // 8)])
    comb_i = jnp.concatenate([low_r * high_i[u:u + 1] + low_i * high_r[u:u + 1] for u in range(J // 8)])
    shape = (NSUB * RADIX, Q)
    scale = 1.0 / math.sqrt(F)

    def write(table, at, row, rr, ri):
        re = comb_r * rr - comb_i * ri
        im = comb_r * ri + comb_i * rr
        re_b, im_b = re.astype(BF), im.astype(BF)
        table[at, row:row + J, :Q] = re_b
        table[at, row:row + J, Q:] = (-im).astype(BF)
        table[at, row + J:row + 2 * J, :Q] = im_b
        table[at, row + J:row + 2 * J, Q:] = re_b

    for copy in small:
        copy.wait()
    freq = by_subgrid([shifts[0, 0, s] for s in range(NSUB)], shape) + iota(shape, 0) % RADIX
    turn = by_subgrid([phase[0, s] for s in range(NSUB)], shape)
    gain = by_subgrid([cover[0, s].astype(F32) * scale for s in range(NSUB)], shape)
    row_r, row_i = unit(freq * (iota(shape, 1) + h * (F // 2)) - turn)
    row_r, row_i = row_r * gain, row_i * gain
    for s in range(NSUB):
        for t in range(RADIX):
            n = s * RADIX + t
            write(left, (shifts[0, 0, s] + t) & 3, s * 2 * J, row_r[n:n + 1], row_i[n:n + 1])
    freq = by_subgrid([shifts[0, 1, s] for s in range(NSUB)], shape) + iota(shape, 0) % RADIX
    row_r, row_i = unit(freq * iota(shape, 1))
    row_r, row_i = row_r * scale, row_i * scale
    for n in range(NSUB * RADIX):
        at = n // RADIX * RADIX + ((shifts[0, 1, n // RADIX] + n) & 3)
        write(right, at, 0, row_r[n:n + 1], row_i[n:n + 1])

    for q in range(F // 2 // LANES):
        row = taper[pl.ds(h * 4 + q, 1), :]
        columns[q * LANES:(q + 1) * LANES, :] = jnp.transpose(jnp.broadcast_to(row, (LANES, LANES)))

    def butterfly(b, v, across):
        lines = []
        for a in range(2):
            down = columns[pl.ds(a * Q + b, ROWS), :]
            z = []
            for c in range(RADIX):
                weight = down * across[c]
                lane = c * Q + v * LANES
                z.append([
                    facet[p, pl.ds(a * Q + b, ROWS), lane:lane + LANES].astype(F32) * weight
                    for p in range(2)
                ])
            e0 = [z[0][p] + z[2][p] for p in range(2)]
            e1 = [z[0][p] - z[2][p] for p in range(2)]
            o0 = [z[1][p] + z[3][p] for p in range(2)]
            o1 = [z[1][p] - z[3][p] for p in range(2)]
            lines.append([
                (e0[0] + o0[0], e0[1] + o0[1]),
                (e1[0] + o1[1], e1[1] - o1[0]),
                (e0[0] - o0[0], e0[1] - o0[1]),
                (e1[0] - o1[1], e1[1] + o1[0]),
            ])
        for c in range(RADIX):
            (ar, ai), (br, bi) = lines[0][c], lines[1][c]
            lane = (v * RADIX + c) * LANES
            outs = [(ar + br, ai + bi), (ar + bi, ai - br), (ar - br, ai - bi), (ar - bi, ai + br)]
            for x, pair in enumerate(outs):
                for p in range(2):
                    grid[x, pl.ds(p * Q + b, ROWS), lane:lane + LANES] = pair[p].astype(BF)

    def first(c, v, y):
        lane = (v * RADIX + y) * LANES
        sums = jnp.dot(left[c], grid[c, :, lane:lane + 2 * LANES], preferred_element_type=F32).astype(BF)
        for s in range(NSUB):
            for p in range(2):
                row = (2 * s + p) * J
                for i in range(2):
                    to = (2 * (y + i) + p) * Q + v * LANES
                    part[s, c, :, to:to + LANES] = sums[row:row + J, i * LANES:(i + 1) * LANES]

    def rim(v):
        return [jnp.broadcast_to(taper[2 * a + v:2 * a + v + 1, :], (ROWS, LANES)) for a in range(RADIX)]

    blocks = Q // ROWS
    edges = rim(0)
    for copy in copies:
        copy.wait()
    for i in range(blocks):
        butterfly(i * ROWS, 0, edges)
    tiles = [(c, y) for c in range(RADIX) for y in (0, 2)]
    edges = rim(1)
    for n, (c, y) in enumerate(tiles):
        for i in range(n * blocks // len(tiles), (n + 1) * blocks // len(tiles)):
            butterfly(i * ROWS, 1, edges)
        first(c, 0, y)
    for c, y in tiles:
        first(c, 1, y)

    second(1 - h, shifts, owner, right, part, strips, send)


def kept(shifts_in, owner_in, right, part, keep, shifts, owner, strips, sem):
    copies = [
        pltpu.make_async_copy(src, dst, sem.at[n])
        for n, (src, dst) in enumerate([(shifts_in, shifts), (owner_in, owner)])
    ]
    for copy in copies:
        copy.start()
    for copy in copies:
        copy.wait()
    second(lax.axis_index("row"), shifts, owner, right, part, strips, keep)


def column(parts, out):
    depth = out.shape[0]
    for z in range(depth):
        sums = [parts[i + z].astype(F32) for i in range(0, STRIPS, depth)]
        while len(sums) > 1:
            sums = [a + b for a, b in zip(sums[::2], sums[1::2])]
        out[z] = sums[0].astype(BF)


def total(parts, out):
    lane, col = iota((LANES, 2 * SG), 0), iota((LANES, 2 * SG), 1)
    spread = (col == (lane // J) * SG + (lane % J) * RADIX).astype(F32).astype(BF)
    sums = [parts[i].astype(F32) for i in range(parts.shape[0])]
    while len(sums) > 1:
        sums = [a + b for a, b in zip(sums[::2], sums[1::2])]
    high = sums[0].astype(BF)
    rest = sums[0] - high.astype(F32)
    middle = rest.astype(BF)
    low = (rest - middle.astype(F32)).astype(BF)
    wide = jnp.dot(jnp.concatenate([high, middle, low]), spread, preferred_element_type=F32)
    wide = wide[:ROWS] + (wide[ROWS:2 * ROWS] + wide[2 * ROWS:])
    result = wide[:RADIX]
    for k in range(1, RADIX):
        result = result + pltpu.roll(wide[k * RADIX:(k + 1) * RADIX], k, 1)
    out[0] = result


def per_device(facet, taper, shifts, cover, phase, owner):
    anywhere = pl.BlockSpec(memory_space=pl.ANY)
    vmem = pl.BlockSpec(memory_space=pltpu.VMEM)
    strips = (STRIPS, ROWS, LANES)
    given = [
        pltpu.with_memory_space_constraint(x, pltpu.HBM)
        for x in (shifts, cover, phase, owner, taper.reshape(8, LANES), facet)
    ]
    held = pltpu.VMEM((NSUB, (HALF + 1) * ROWS, LANES), F32)
    send, part, right = pl.pallas_call(
        images,
        out_shape=(
            jax.ShapeDtypeStruct(strips, BF),
            jax.ShapeDtypeStruct((NSUB, RADIX, J, 2 * F), BF),
            jax.ShapeDtypeStruct((NSUB * RADIX, 2 * J, 2 * Q), BF),
        ),
        in_specs=[anywhere] * 6,
        out_specs=(vmem, vmem, vmem),
        scratch_shapes=[
            pltpu.SMEM(shifts.shape, jnp.int32),
            pltpu.SMEM(cover.shape, jnp.int32),
            pltpu.SMEM(phase.shape, jnp.int32),
            pltpu.SMEM(owner.shape, jnp.int32),
            pltpu.VMEM((8, LANES), F32),
            pltpu.VMEM((2, F // 2, F), BF),
            pltpu.VMEM((RADIX, 2 * Q, F), BF),
            pltpu.VMEM((RADIX, NSUB * 2 * J, 2 * Q), BF),
            held,
            pltpu.VMEM((F // 2, LANES), F32),
            pltpu.SemaphoreType.DMA((7,)),
        ],
        compiler_params=pltpu.CompilerParams(vmem_limit_bytes=32 * 2**20),
        name="images",
    )(*given)
    with jax.named_scope("row_swap"):
        other = lax.ppermute(send, "row", [(0, 1), (1, 0)])
    work = 2 * STRIPS * ROWS * LANES * 2 * Q
    keep = pl.pallas_call(
        kept,
        out_shape=jax.ShapeDtypeStruct(strips, F32),
        in_specs=[anywhere, anywhere, vmem, vmem],
        out_specs=vmem,
        scratch_shapes=[
            pltpu.SMEM(shifts.shape, jnp.int32),
            pltpu.SMEM(owner.shape, jnp.int32),
            held,
            pltpu.SemaphoreType.DMA((2,)),
        ],
        compiler_params=pltpu.CompilerParams(vmem_limit_bytes=16 * 2**20),
        cost_estimate=pl.CostEstimate(flops=work, bytes_accessed=6 * 2**20, transcendentals=0),
        name="kept",
    )(given[0], given[3], *(pltpu.with_memory_space_constraint(x, pltpu.VMEM) for x in (right, part)))
    with jax.named_scope("row_swap"):
        merged = (keep + other.astype(F32)).astype(BF)
    with jax.named_scope("to_columns"):
        parts = lax.all_to_all(merged, "plane", split_axis=0, concat_axis=0, tiled=True)
    depth = lax.axis_size("line")
    summed = pl.pallas_call(
        column,
        out_shape=pltpu.VMEM((depth, ROWS, LANES), BF),
        in_specs=[vmem],
        out_specs=vmem,
        name="column",
    )(pltpu.with_memory_space_constraint(parts, pltpu.VMEM))
    with jax.named_scope("to_owners"):
        parts = lax.all_to_all(summed, "line", split_axis=0, concat_axis=0, tiled=True)
    return pl.pallas_call(
        total,
        out_shape=jax.ShapeDtypeStruct((1, RADIX, 2 * SG), F32),
        in_specs=[vmem],
        out_specs=vmem,
        name="total",
    )(pltpu.with_memory_space_constraint(parts, pltpu.VMEM))


def solution(mesh):
    line = 8
    grid = Mesh(mesh.devices.reshape(-1, line, mesh.devices.shape[1]), ("plane", "line", "row"))
    facet = ("plane", "line")
    return jax.shard_map(
        per_device,
        mesh=grid,
        in_specs=(
            P(facet, None, "row", None),
            P(),
            P(facet, None, None),
            P(facet, None),
            P(facet, None),
            P(),
        ),
        out_specs=P(facet, "row", None),
        check_vma=False,
    )
```
